512 devices in a mesh: stratum: 128 (over y, z_lo, x), rep: 4 (over z_hi, core).
Axes of the slice: x: 4, y: 8, z: 8 (z_hi: 2, z_lo: 4; z = z_hi * 4 + z_lo), core: 2. Of those that a mesh axis runs over, the one named last changes fastest.
Arguments:
- user_rows: float32 [524288, 256], P(('stratum', 'rep')), may hold values from -1.5 to 1.5
- user_accum: float32 [524288], P(('stratum', 'rep')), may hold values from 4 to 400
- item_rows: float32 [65536, 256], P('stratum'), may hold values from -1.5 to 1.5
- item_accum: float32 [65536, 256], P('stratum'), may hold values from 30 to 3000
- move_lists: int32 [3, 128], replicated, may hold values from 0 to 127, each once within a row
- tile_lists: int32 [3, 128, 4, 32], P(None, 'stratum', 'rep'), may hold values from 0 to 31, each once within a row
- tile_counts: int32 [3, 128, 4], P(None, 'stratum', 'rep'), may hold values from 4 to 32, as said below
- rating_bits: int32 [3, 128, 4, 32, 16, 128], P(None, 'stratum', 'rep'), may hold values from 0 to 255
Outputs:
- new_users: float32 [524288, 256], P(('stratum', 'rep'))
- new_items: float32 [65536, 256], P('stratum')
The draws below stay inside these ranges and needn't reach their ends.
Inputs may be any that keep to these rules, and one draw needn't show every extreme that they name: `move_lists`: each row is a permutation of the 128 block positions. `tile_lists`: each list is a permutation of the 32 slots; only its first tile_counts entries are used. `tile_counts`: in every stratum some pair uses all 32 slots.
All inputs are finite; a program needn't handle non-finite values.
Results may differ from the reference program's by a relative error of at most 0.011.
Values may be sent and summed in bfloat16 or wider, within the bound.
A program may use at most 64 MiB of HBM per device.

```python
import math
import jax
import jax.numpy as jnp
from jax import lax

R = 256
TILE = 128
ROW_TILES = 8
COL_TILES = 4
STRATA = 3
WORDS = 16
SLOTS = 32
U_DEV = 1024
BLK = 512
BLOCKS = 128
REPS = 4
USERS = 524288
ITEMS = 65536


def draw_tile_counts(key, part):
    key = jax.random.fold_in(key, 11)
    raw_picks = jax.random.randint(key, (STRATA, BLOCKS * REPS), 1, SLOTS + 1)
    counts = jnp.maximum(max(1, SLOTS // 8), raw_picks * raw_picks // SLOTS)
    chosen = jax.random.randint(jax.random.fold_in(key, 1), (STRATA, 1), 0, BLOCKS * REPS)
    filled = jnp.where(jnp.arange(BLOCKS * REPS)[None, :] == chosen, SLOTS, counts)
    return filled.reshape(STRATA, BLOCKS, REPS).astype(jnp.int32)


def with_ends(result, stream_key, low, high):
    extent = result.shape
    place = [jax.random.randint(jax.random.fold_in(stream_key, axis), (), 0, extent[axis]) for axis in range(len(extent))]
    result = result.at[tuple(place)].set(low)
    longest = extent.index(max(extent))
    place[longest] = (place[longest] + 1) % extent[longest]
    return result.at[tuple(place)].set(high)


def level_of(key, shape, cuts, low, high):
    def one(axis_at, parts):
        steps = jax.random.uniform(jax.random.fold_in(jax.random.fold_in(key, 6), axis_at), (parts,), jnp.float32, low / len(cuts), high / len(cuts))
        return jnp.repeat(jnp.exp(steps), shape[axis_at] // parts).reshape((-1,) + (1,) * (len(shape) - axis_at - 1))

    level = one(*cuts[0])
    for cut in cuts[1:]:
        level = level * one(*cut)
    return level


def centred(key, extent, scale, most, split=(), kind=jnp.bfloat16):
    array = scale * jax.random.normal(key, extent, jnp.float32)
    if split:
        array = array * level_of(key, extent, split, -0.22, 0.18)
    return jnp.clip(array, -most, most).astype(kind)


def setup_inputs(seed: int = 0) -> dict:
    key_of = jax.random.split(jax.random.key(seed), 9)
    return {
        "user_rows": centred(key_of[0], (USERS, R), 0.25, 1.5, ((0, 512),), jnp.float32),
        "user_accum": jnp.clip(jnp.exp(math.log(400.0) - 4.6051702 * jax.random.uniform(key_of[1], (USERS,), jnp.float32) ** level_of(key_of[1], (USERS,), ((0, 512),), -0.2, 0.2)), 4.0, 400.0),
        "item_rows": centred(key_of[2], (ITEMS, R), 0.25, 1.5, ((0, 128),), jnp.float32),
        "item_accum": jnp.clip(jnp.exp(math.log(3000.0) - 4.6051702 * jax.random.uniform(key_of[3], (ITEMS, R), jnp.float32) ** level_of(key_of[3], (ITEMS, R), ((0, 128),), -0.2, 0.2)), 30.0, 3000.0),
        "move_lists": jax.vmap(lambda own: jax.random.permutation(own, BLOCKS))(jax.random.split(key_of[4], STRATA)).reshape((STRATA, BLOCKS)).astype(jnp.int32),
        "tile_lists": jax.vmap(lambda own: jax.random.permutation(own, SLOTS))(jax.random.split(key_of[5], STRATA * BLOCKS * REPS)).reshape((STRATA, BLOCKS, REPS, SLOTS)).astype(jnp.int32),
        "tile_counts": draw_tile_counts(jax.random.fold_in(key_of[8], 71), 0),
        "rating_bits": with_ends(jax.random.randint(key_of[7], (STRATA, BLOCKS, REPS, SLOTS, WORDS, TILE), 0, 256), jax.random.fold_in(key_of[7], 1), 0, 255).astype(jnp.int32),
    }


CONFIDENCE = 2.0
SHRINKAGE = 0.02
RATE_START = 0.25
RATE_DECAY = 0.75

def unpack_bits(bit_words):
    shifts = jnp.arange(8, dtype=jnp.int32)
    bit_flags = jnp.bitwise_and(jnp.right_shift(bit_words[:, :, None, :], shifts[None, None, :, None]), 1)
    return bit_flags.reshape(bit_words.shape[0], bit_words.shape[1] * 8, bit_words.shape[2]).astype(jnp.float32)

def invert(targets):
    entries = targets.shape[0]
    numbers = jnp.arange(entries, dtype=jnp.int32)
    return lax.optimization_barrier(jnp.sum(jnp.where(targets[None, :] == numbers[:, None], numbers[None, :], 0), axis=1)).astype(jnp.int32)

def dense_grid(tile_grid):
    tile_size = tile_grid.shape[1]
    arranged = tile_grid.reshape(ROW_TILES, COL_TILES, tile_size, tile_size)
    return jnp.transpose(arranged, (0, 3, 1, 2)).reshape(ROW_TILES * tile_size, COL_TILES * tile_size)

def slab_terms(user_slab, item_low, tile_list, tile_count, bit_words):
    slot_total = tile_list.shape[0]
    numbers = jnp.arange(slot_total, dtype=jnp.int32)
    active = (numbers < tile_count).astype(jnp.float32)
    onehot = (tile_list[:, None] == numbers[None, :]).astype(jnp.float32) * active[:, None]
    observed = unpack_bits(bit_words)
    tile_grid = jnp.einsum('js,jab->sab', onehot, observed, precision=lax.Precision.HIGHEST)
    used_tiles = lax.optimization_barrier(jnp.sum(onehot, axis=0))
    tile_size = bit_words.shape[2]
    used_grid = jnp.broadcast_to(used_tiles[:, None, None], (slot_total, tile_size, tile_size))
    target = dense_grid(tile_grid)
    used_dense = dense_grid(used_grid)
    user_low = user_slab.astype(jnp.bfloat16)
    scores = jnp.dot(user_low, item_low.T, preferred_element_type=jnp.float32)
    residual = (used_dense * (1.0 + CONFIDENCE * target) * (scores - target)).astype(jnp.bfloat16)
    user_grad = jnp.dot(residual, item_low, preferred_element_type=jnp.float32) + SHRINKAGE * user_slab
    item_part = jnp.dot(residual.T, user_low, preferred_element_type=jnp.float32)
    return (user_grad, item_part)

def reference(user_rows, user_accum, item_rows, item_accum, move_lists, tile_lists, tile_counts, rating_bits):
    user_state = user_rows.reshape(BLOCKS, REPS, U_DEV, R)
    user_acc = user_accum.reshape(BLOCKS, REPS, U_DEV)
    item_state = item_rows.reshape(BLOCKS, BLK, R)
    item_acc = item_accum.reshape(BLOCKS, BLK, R)
    for stratum_idx in range(STRATA):
        step_rate = RATE_START * RATE_DECAY ** stratum_idx
        sources = invert(move_lists[stratum_idx])
        item_state = jnp.take(item_state, sources, axis=0)
        item_acc = jnp.take(item_acc, sources, axis=0)

        def per_block(packed):
            user_slabs, slab_acc, item_block, block_acc, list_rows, counts, word_rows = packed
            item_low = item_block.astype(jnp.bfloat16)
            item_total = jnp.zeros(item_block.shape, jnp.float32)
            new_slabs = []
            new_accs = []
            for member in range(REPS):
                user_slab = user_slabs[member]
                user_grad, item_part = slab_terms(user_slab, item_low, list_rows[member], counts[member], word_rows[member])
                item_total = item_total + item_part
                acc_next = slab_acc[member] + lax.optimization_barrier(jnp.mean(user_grad * user_grad, axis=1))
                new_accs.append(acc_next)
                new_slabs.append(user_slab - step_rate * user_grad / jnp.sqrt(acc_next)[:, None])
            item_grad = item_total + SHRINKAGE * item_block
            block_next_acc = block_acc + item_grad * item_grad
            block_next = item_block - step_rate * item_grad / jnp.sqrt(block_next_acc)
            return (jnp.stack(new_slabs), jnp.stack(new_accs), block_next, block_next_acc)
        user_state, user_acc, item_state, item_acc = lax.map(per_block, (user_state, user_acc, item_state, item_acc, tile_lists[stratum_idx], tile_counts[stratum_idx], rating_bits[stratum_idx]))
    return (user_state.reshape(USERS, R), item_state.reshape(ITEMS, R))
```

```python
import jax
import jax.numpy as jnp
from jax import lax
from jax.experimental import pallas as pl
from jax.experimental.pallas import tpu as pltpu
from jax.sharding import PartitionSpec as P

STRATA = 3
SHRINKAGE = 0.02
RATE_START = 0.25
RATE_DECAY = 0.75

NX, NY, NZ = 4, 8, 4
POS = NX * NY * NZ
SEMS = 176

F32 = jnp.float32
BF16 = jnp.bfloat16
MESH = pl.DeviceIdType.MESH
NT = (((1,), (1,)), ((), ()))
TN = (((0,), (0,)), ((), ()))


def dot(a, b):
    return jnp.dot(a, b, preferred_element_type=F32)


def iota(shape, axis):
    return lax.broadcasted_iota(jnp.int32, shape, axis)


def order_a(o):
    return ((o // 4) % 4) * 32 + (o // 16) * 4 + o % 4


def order_b(o):
    return ((o // 4) % 8) * 16 + (o % 4) * 4 + o // 32


def kernel(
    user_hbm, uacc_ref, item_hbm, iacc_hbm, move_ref, list_ref, count_ref, bits_hbm,
    user_out, item_out,
    xs, xl, ucol, words, cat, wsort, usort, mask, err, part, yl, yh, ah, onehot, perm, rows_in, acc_in, items_new,
    sp_s, sp_zr, sp_yr, sp_xr,
    ac_s, ac_zr, ac_yr, ac_xr,
    ou_s, ou_xr, ou_yr, ou_cr,
    fa_s, fa_xr, fa_yr, fa_zr,
    bk_cr, bk_z, bk_zr, bk_s, bk_yr, bk_xr,
    fin_s, fin_r, fin_new,
    local_sem, send_sem, recv_sem,
):
    s = lax.axis_index("stratum")
    r = lax.axis_index("rep")
    x = lax.rem(s, 4)
    zl = lax.rem(s // 4, 4)
    y = s // 16
    c = lax.rem(r, 2)
    zh = r // 2
    z = zh * 4 + zl

    def dev_x(v):
        return (y * 16 + zl * 4 + v, r)

    def dev_y(v):
        return (v * 16 + zl * 4 + x, r)

    def dev_zl(v):
        return (y * 16 + v * 4 + x, r)

    def dev_z(v):
        return (y * 16 + lax.rem(v, 4) * 4 + x, (v // 4) * 2 + c)

    other_core = (s, zh * 2 + (1 - c))
    other_zh = (s, (1 - zh) * 2 + c)

    used = [0]
    pending = []

    def send(src, dst, device):
        k = used[0]
        used[0] = k + 1
        copy = pltpu.make_async_remote_copy(
            src_ref=src, dst_ref=dst, send_sem=send_sem.at[k], recv_sem=recv_sem.at[k],
            device_id=device, device_id_type=MESH,
        )
        copy.start()
        pending.append(copy)
        return copy

    far_first = {4: (2, 1, 3), 8: (4, 3, 5, 2, 6, 1, 7)}

    def exchange(n, me, device_of, src_at, recv):
        copies = {}
        for k in far_first[n]:
            peer = lax.rem(me + k, n)
            copies[k] = send(src_at(peer), recv.at[me], device_of(peer))
        recv[me] = src_at(me)[...]
        return copies

    def arrive(copies):
        for k in sorted(copies, key=lambda k: min(k, len(copies) + 1 - k)):
            copies[k].wait_recv()

    def drain():
        for copy in pending:
            copy.wait_send()
        pending.clear()

    quarter = pl.multiple_of(c * 256 + zh * 128, 128)
    loads = [
        pltpu.make_async_copy(item_hbm.at[pl.ds(quarter, 128)], rows_in, local_sem.at[0]),
        pltpu.make_async_copy(iacc_hbm.at[pl.ds(quarter, 128)], acc_in, local_sem.at[1]),
        pltpu.make_async_copy(user_hbm, xs, local_sem.at[2]),
    ] + [
        pltpu.make_async_copy(bits_hbm.at[t, 0, 0], words.at[t], local_sem.at[3 + t]) for t in range(STRATA)
    ]
    for load in loads:
        load.start()

    barrier = pltpu.get_barrier_semaphore()
    peers = (
        [dev_x(lax.rem(x + k, 4)) for k in range(1, 4)]
        + [dev_y(lax.rem(y + k, 8)) for k in range(1, 8)]
        + [dev_z(lax.rem(z + k, 8)) for k in range(1, 8)]
        + [other_core]
    )
    for peer in peers:
        pl.semaphore_signal(barrier, inc=1, device_id=peer, device_id_type=MESH)

    row = iota((POS, POS), 0)
    col = iota((POS, POS), 1)
    perm[0] = (order_a(row) == col).astype(BF16)
    perm[1] = (order_b(row) == col).astype(BF16)

    def reorder(which, array):
        return dot(perm[which], array).astype(BF16)

    loads[0].wait()
    sp_s[0] = rows_in[...].astype(BF16).reshape(4, 32, 256)
    pl.semaphore_wait(barrier, len(peers))

    rows_z = exchange(4, zl, dev_zl, lambda v: sp_s.at[0, v], sp_zr)
    loads[1].wait()
    ac_s[0] = acc_in[...].astype(BF16).reshape(4, 32, 256)
    accs_z = exchange(4, zl, dev_zl, lambda v: ac_s.at[0, v], ac_zr)

    chain = (order_b(col) == row).astype(BF16)
    for t in range(STRATA):
        move = move_ref[pl.ds(t, 1), :]
        onehot[t] = dot((move == order_b(row)).astype(BF16), chain).astype(BF16)
        if t + 1 < STRATA:
            chain = dot((move == row).astype(BF16), chain).astype(BF16)

    arrive(rows_z)
    sp_s[1] = reorder(0, sp_zr[...].reshape(POS, 256)).reshape(4, 32, 256)
    rows_y = exchange(8, y, dev_y, lambda v: sp_s.at[1, v // 2, pl.ds(pl.multiple_of(lax.rem(v, 2) * 16, 16), 16)], sp_yr)
    arrive(accs_z)
    ac_s[1] = reorder(0, ac_zr[...].reshape(POS, 256)).reshape(4, 32, 256)
    accs_y = exchange(8, y, dev_y, lambda v: ac_s.at[1, v // 2, pl.ds(pl.multiple_of(lax.rem(v, 2) * 16, 16), 16)], ac_yr)

    loads[2].wait()
    xl[...] = xs[...].astype(BF16)
    for a in range(8):
        line = jnp.broadcast_to(uacc_ref[pl.ds(a, 1), :], (128, 128))
        ucol[pl.ds(a * 128, 128), :] = jnp.sum(jnp.where(row == col, line, 0.0), axis=1, keepdims=True)

    def sort_words(t):
        loads[3 + t].wait()
        cat[:, 0:128] = words[t].reshape(512, 128).astype(F32).astype(BF16)
        cat[:, 128:256] = jnp.ones((512, 128), BF16)
        spread = (iota((32, 512), 1) // 16 == iota((32, 512), 0)).astype(BF16)
        slots = jnp.broadcast_to(list_ref[t, 0].astype(F32).astype(BF16), (8, 32))
        slot_of = dot(slots, spread)[0:1, :].astype(jnp.int32)
        lane = iota((1, 512), 1)
        slot_of = jnp.where(lane // 16 < count_ref[t, 0, 0], slot_of * 16 + lane % 16, -1)
        for a in range(4):
            pick = (slot_of == iota((128, 512), 0) + a * 128).astype(BF16)
            got = dot(pick, cat[...])
            wsort[pl.ds(a * 128, 128), :] = got[:, 0:128].astype(jnp.int32)
            usort[pl.ds(a * 128, 128), :] = got[:, 128:256]

    def fill_mask():
        shift = iota((8, 128), 0)

        def one_slot(slot, carry):
            base = slot * 16
            at_row = pl.multiple_of(lax.rem(slot, 4) * 128, 128)
            at_col = pl.multiple_of((slot // 4) * 128, 128)
            on = jnp.broadcast_to(usort[pl.ds(base, 1), :], (8, 128))
            for w in range(0, 16, 2):
                both = []
                for v in (w, w + 1):
                    line = jnp.broadcast_to(wsort[pl.ds(base + v, 1), :], (8, 128))
                    bit = jnp.bitwise_and(jnp.right_shift(line, shift), 1).astype(F32)
                    both.append(on + 2.0 * bit)
                mask[pl.ds(at_row + w * 8, 16), pl.ds(at_col, 128)] = jnp.concatenate(both, axis=0).astype(BF16)
            return carry

        lax.fori_loop(0, 32, one_slot, 0)

    arrive(rows_y)
    sp_s[2] = reorder(1, sp_yr[...].reshape(POS, 256)).reshape(4, 32, 256)
    rows_x = exchange(4, x, dev_x, lambda v: sp_s.at[2, v], sp_xr)
    arrive(accs_y)
    ac_s[2] = reorder(1, ac_yr[...].reshape(POS, 256)).reshape(4, 32, 256)
    accs_x = exchange(4, x, dev_x, lambda v: ac_s.at[2, v], ac_xr)
    sort_words(0)
    arrive(rows_x)
    home = sp_xr[...].reshape(POS, 256)
    yh[...] = home.astype(F32)

    for t in range(STRATA):
        last = t == STRATA - 1
        rate = RATE_START * RATE_DECAY**t
        ou_s[t, 0] = dot(onehot[t], yh[...].astype(BF16)).astype(BF16).reshape(4, 32, 256)
        out_x = exchange(4, x, dev_x, lambda v: ou_s.at[t, 0, v], ou_xr.at[t])
        if last:
            fa_s[0] = dot(onehot[t], ah[...].astype(BF16)).astype(BF16).reshape(4, 32, 256)
            fa_x = exchange(4, x, dev_x, lambda v: fa_s.at[0, v], fa_xr)
        if t == 0:
            arrive(accs_x)
            ah[...] = ac_xr[...].reshape(POS, 256).astype(F32)
            fill_mask()
        drain()
        arrive(out_x)
        ou_s[t, 1] = reorder(0, ou_xr[t].reshape(POS, 256)).reshape(4, 32, 256)
        out_y = exchange(
            8, y, dev_y, lambda v: ou_s.at[t, 1, v // 2, pl.ds(pl.multiple_of(lax.rem(v, 2) * 16, 16), 16)], ou_yr.at[t]
        )
        if last:
            arrive(fa_x)
            fa_s[1] = reorder(0, fa_xr[...].reshape(POS, 256)).reshape(4, 32, 256)
        arrive(out_y)
        ou_s[t, 2] = reorder(1, ou_yr[t].reshape(POS, 256)).reshape(4, 32, 256)
        half = yl.at[t, c]
        out_z = exchange(8, z, dev_z, lambda v: ou_s.at[t, 2, lax.rem(v, 4)], half)
        if last:
            fa_y = exchange(
                8, y, dev_y, lambda v: fa_s.at[1, v // 2, pl.ds(pl.multiple_of(lax.rem(v, 2) * 16, 16), 16)], fa_yr
            )
        over = [send(half.at[z], yl.at[t, c, z], other_core)]
        for k in (1, 7, 2, 6, 3, 5, 4):
            out_z[k].wait_recv()
            piece = lax.rem(z + 8 - k, 8)
            over.append(send(half.at[piece], yl.at[t, c, piece], other_core))
        if last:
            arrive(fa_y)
            fa_s[2] = reorder(1, fa_yr[...].reshape(POS, 256)).reshape(4, 32, 256)
            fa_z = exchange(4, zl, dev_zl, lambda v: fa_s.at[2, v], fa_zr)
        for copy in over:
            copy.wait_recv()

        def item_chunk(h, q):
            items = yl[t, h, pl.ds(q * 4, 4)].reshape(128, 256)
            at = pl.multiple_of(h * 256 + q * 128, 128)
            scores = lax.dot_general(items, xl[...], NT, preferred_element_type=F32)
            weight = mask[pl.ds(at, 128), :].astype(F32)
            e = (weight * (scores - jnp.where(weight > 2.0, 1.0, 0.0))).astype(BF16)
            err[pl.ds(at, 128), :] = e
            return dot(e, xl[...])

        for q in range(2):
            part[0, pl.ds(q * 128, 128), :] = item_chunk(1 - c, q)
        swap = send(part.at[0], bk_cr.at[t], other_core)
        for q in range(2):
            part[1, pl.ds(q * 128, 128), :] = item_chunk(c, q)
        swap.wait_recv()
        both = part[1] + bk_cr[t]

        def users():
            items = yl[t].reshape(512, 256)
            for u in range(4):
                at = pl.ds(u * 256, 256)
                old = xs[at, :]
                grad = lax.dot_general(err[:, u * 256 : u * 256 + 256], items, TN, preferred_element_type=F32)
                grad = grad + SHRINKAGE * old
                acc = ucol[at, :] + jnp.sum(grad * grad, axis=1, keepdims=True) * (1.0 / 256.0)
                ucol[at, :] = acc
                new = old - grad * (rate / jnp.sqrt(acc))
                xs[at, :] = new
                if not last:
                    xl[at, :] = new.astype(BF16)

        if not last:
            bk_z[t] = both.astype(BF16).reshape(8, 32, 256)
            back_z = exchange(8, z, dev_z, lambda v: bk_z.at[t, v], bk_zr.at[t])
            users()
            drain()
            arrive(back_z)
            near = bk_zr[t, 0:4].reshape(POS, 256)
            away = bk_zr[t, 4:8].reshape(POS, 256)
            bk_s[t, 0] = (dot(perm[0], near) + dot(perm[0], away)).astype(BF16).reshape(4, 32, 256)
            back_y = exchange(
                8, y, dev_y, lambda v: bk_s.at[t, 0, v // 2, pl.ds(pl.multiple_of(lax.rem(v, 2) * 16, 16), 16)], bk_yr.at[t]
            )
            sort_words(t + 1)
            arrive(back_y)
            bk_s[t, 1] = reorder(1, bk_yr[t].reshape(POS, 256)).reshape(4, 32, 256)
            back_x = exchange(4, x, dev_x, lambda v: bk_s.at[t, 1, v], bk_xr.at[t])
            fill_mask()
            arrive(back_x)
            grad = lax.dot_general(onehot[t], bk_xr[t].reshape(POS, 256), TN, preferred_element_type=F32)
            grad = grad + SHRINKAGE * yh[...]
            acc = ah[...] + grad * grad
            ah[...] = acc
            yh[...] = yh[...] - rate * grad / jnp.sqrt(acc)
        else:
            part[1] = both
            fin_s[...] = part[1, pl.ds(pl.multiple_of((1 - zh) * 128, 128), 128), :].astype(BF16)
            cross = send(fin_s, fin_r, other_zh)
            users()
            store = pltpu.make_async_copy(xs, user_out, local_sem.at[6])
            store.start()
            arrive(fa_z)
            old = yl[t, c, pl.ds(zh * 4, 4)].reshape(128, 256).astype(F32)
            before = fa_zr[...].reshape(128, 256).astype(F32)
            cross.wait_recv()
            grad = part[1, pl.ds(pl.multiple_of(zh * 128, 128), 128), :] + fin_r[...].astype(F32)
            grad = grad + SHRINKAGE * old
            new = old - rate * grad / jnp.sqrt(before + grad * grad)
            fin_new[c, zh] = new.astype(BF16)
            mine = fin_new.at[c, zh]
            gather = [send(mine, fin_new.at[c, zh], other_zh), send(mine, fin_new.at[c, zh], other_core)]
            gather[0].wait_recv()
            theirs = fin_new.at[c, 1 - zh]
            gather.append(send(theirs, fin_new.at[c, 1 - zh], other_core))
            drain()
            gather[1].wait_recv()
            gather[2].wait_recv()
            items_new[...] = fin_new[...].reshape(512, 256).astype(F32)
            done = pltpu.make_async_copy(items_new, item_out, local_sem.at[7])
            done.start()
            store.wait()
            done.wait()


def on_device(
    user_rows, user_accum, item_rows, item_accum, move_lists, tile_lists, tile_counts, rating_bits
):
    vmem, smem, anywhere = (
        pl.BlockSpec(memory_space=pltpu.VMEM), pl.BlockSpec(memory_space=pltpu.SMEM), pl.BlockSpec(memory_space=pl.ANY),
    )
    v = pltpu.VMEM
    stage, wide = (4, 32, 256), (8, 16, 256)
    new_users, new_items = pl.pallas_call(
        kernel,
        out_shape=(
            jax.ShapeDtypeStruct((1024, 256), F32),
            jax.ShapeDtypeStruct((512, 256), F32),
        ),
        in_specs=[anywhere, vmem, anywhere, anywhere, vmem, vmem, smem, anywhere],
        out_specs=(anywhere, anywhere),
        scratch_shapes=[
            v((1024, 256), F32), v((1024, 256), BF16), v((1024, 1), F32),
            v((STRATA, 32, 16, 128), jnp.int32), v((512, 256), BF16), v((512, 128), jnp.int32), v((512, 128), F32),
            v((512, 1024), BF16), v((512, 1024), BF16), v((2, 256, 256), F32), v((STRATA, 2, 8, 32, 256), BF16),
            v((POS, 256), F32), v((POS, 256), F32), v((STRATA, POS, POS), BF16), v((2, POS, POS), BF16),
            v((128, 256), F32), v((128, 256), F32), v((512, 256), F32),
            v((3, *stage), BF16), v(stage, BF16), v(wide, BF16), v(stage, BF16),
            v((3, *stage), BF16), v(stage, BF16), v(wide, BF16), v(stage, BF16),
            v((STRATA, 3, *stage), BF16), v((STRATA, *stage), BF16), v((STRATA, *wide), BF16), v((8, 128), F32),
            v((3, *stage), BF16), v(stage, BF16), v(wide, BF16), v(stage, BF16),
            v((STRATA, 256, 256), F32), v((2, 8, 32, 256), BF16), v((2, 8, 32, 256), BF16),
            v((2, 2, *stage), BF16), v((2, *wide), BF16), v((2, *stage), BF16),
            v((128, 256), BF16), v((128, 256), BF16), v((2, 2, 128, 256), BF16),
            pltpu.SemaphoreType.DMA((8,)),
            pltpu.SemaphoreType.DMA((SEMS,)),
            pltpu.SemaphoreType.DMA((SEMS,)),
        ],
        compiler_params=pltpu.CompilerParams(
            collective_id=0, has_side_effects=True, vmem_limit_bytes=48 * 1024 * 1024
        ),
        cost_estimate=pl.CostEstimate(flops=3 * 3 * 2 * 1024 * 512 * 256, bytes_accessed=6 * 1024 * 1024, transcendentals=0),
    )(user_rows, user_accum.reshape(8, 128), item_rows, item_accum, move_lists, tile_lists, tile_counts, rating_bits)
    return new_users, new_items


def solution(mesh):
    in_specs = (
        P(("stratum", "rep"), None),
        P(("stratum", "rep")),
        P("stratum", None),
        P("stratum", None),
        P(),
        P(None, "stratum", "rep", None),
        P(None, "stratum", "rep"),
        P(None, "stratum", "rep", None, None, None),
    )
    out_specs = (P(("stratum", "rep"), None), P("stratum", None))
    return jax.shard_map(
        on_device, mesh=mesh, in_specs=in_specs, out_specs=out_specs, check_vma=False
    )
```

```python
import jax
import jax.numpy as jnp
from jax import lax
from jax.experimental import pallas as pl
from jax.experimental.pallas import tpu as pltpu
from jax.sharding import PartitionSpec as P

STRATA = 3
SHRINKAGE = 0.02
RATE_START = 0.25
RATE_DECAY = 0.75

F32 = jnp.float32
BF16 = jnp.bfloat16
MESH = pl.DeviceIdType.MESH
NT = (((1,), (1,)), ((), ()))
TN = (((0,), (0,)), ((), ()))
X_ORDER = (0, 1, 3, 2)


def dot(a, b):
    return jnp.dot(a, b, preferred_element_type=F32)


def iota(shape, axis):
    return lax.broadcasted_iota(jnp.int32, shape, axis)


def natural(d):
    return (d // 16) * 16 + (d % 4) * 4 + (d // 4) % 4


def rows_at(index, size):
    return pl.ds(pl.multiple_of(index * size, size), size)


def kernel(
    user_hbm, uacc_hbm, item_hbm, iacc_hbm, move_hbm, list_hbm, count_ref, bits_hbm,
    user_out, item_out,
    xs, xl, uacc_ref, ucol, move_ref, list_ref, words, cat, wsort, usort, mask, err, yl, part, yh, ah,
    onehot, onehot_t, perm, perm_sum, rows_in, acc_in, items_new,
    sp_n, sp_s, sp_yr, sp_zr,
    ac_n, ac_s, ac_yr, ac_zr,
    ou_s, ou_yr,
    fa_s, fa_yr, fa_zr,
    bk_cr, bk_z, bk_zr, bk_s, bk_yr,
    fin_s, fin_r,
    local_sem, send_sem, recv_sem, line_sem,
):
    s = lax.axis_index("stratum")
    r = lax.axis_index("rep")
    x = lax.rem(s, 4)
    zl = lax.rem(s // 4, 4)
    y = s // 16
    c = lax.rem(r, 2)
    zh = r // 2
    z = zh * 4 + zl
    half = pl.ds(pl.multiple_of(c * 128, 128), 128)
    other_half = pl.ds(pl.multiple_of((1 - c) * 128, 128), 128)

    def dev(xv, yv, zv):
        return (yv * 16 + lax.rem(zv, 4) * 4 + xv, (zv // 4) * 2 + c)

    other_core = (s, zh * 2 + (1 - c))
    other_zh = (s, (1 - zh) * 2 + c)

    loads = []

    def load(src, dst):
        copy = pltpu.make_async_copy(src, dst, local_sem.at[len(loads)])
        loads.append(copy)
        copy.start()
        return copy

    load_rows = load(item_hbm.at[:, half], rows_in)
    load_acc = load(iacc_hbm.at[:, half], acc_in)
    load_move = load(move_hbm, move_ref)
    load_list = load(list_hbm, list_ref)
    load_bits = [load(bits_hbm.at[0, 0, 0], words.at[0])]
    load_uacc = load(uacc_hbm, uacc_ref)
    load_user = load(user_hbm, xs)
    load_bits += [load(bits_hbm.at[t, 0, 0], words.at[t]) for t in (1, 2)]

    barrier = pltpu.get_barrier_semaphore()
    x_peers = [dev(lax.rem(x + k, 4), y, z) for k in (2, 1, 3)]
    y_peers = [dev(x, lax.rem(y + k, 8), z) for k in (4, 3, 5, 2, 6, 1, 7)]
    z_peers = [dev(x, y, lax.rem(z + k, 8)) for k in (4, 3, 5, 2, 6, 1, 7)]
    peers = y_peers + z_peers + x_peers + [other_core]
    for peer in peers:
        pl.semaphore_signal(barrier, inc=1, device_id=peer, device_id_type=MESH)

    sends = []
    arrivals = [0]

    def take(ref):
        k = len(sends)
        sends.append(ref)
        return send_sem.at[k]

    def arrival():
        k = arrivals[0]
        arrivals[0] = k + 1
        return recv_sem.at[k]

    def send(src, dst, sent, landed, device):
        pltpu.make_async_remote_copy(
            src_ref=src, dst_ref=dst, send_sem=sent, recv_sem=landed, device_id=device, device_id_type=MESH
        ).start()

    def wait(ref, sem):
        pltpu.make_async_copy(ref, ref, sem).wait()

    def along_y(src, recv):
        sent, landed = take(recv.at[pl.ds(0, 7)]), arrival()
        for k in (4, 3, 5, 2, 6, 1, 7):
            peer = lax.rem(y + k, 8)
            send(src.at[peer], recv.at[y], sent, landed, dev(x, peer, z))
        recv[y] = src[y]
        return lambda: wait(recv.at[pl.ds(0, 7)], landed)

    def to_homes(src, recv):
        sent, landed = take(recv.at[pl.ds(0, 15)]), arrival()
        here = x * 4 + zl
        for kx in (2, 1, 3, 0):
            for k in (3, 0, 2, 1):
                if kx == 0 and k == 1:
                    continue
                px = lax.rem(x + kx, 4)
                send(src.at[px * 4 + k], recv.at[here], sent, landed, dev(px, y, lax.rem(z + 7 + k, 8)))
        recv[here] = src[x * 4 + 1]
        return lambda: wait(recv.at[pl.ds(0, 15)], landed)

    far_z = (4, 3, 5, 2, 6, 1, 7)

    def to_positions(src, recv, whole):
        sent = take(recv.at[pl.ds(0, 31 * 16), pl.ds(0, 128)] if whole else recv.at[pl.ds(0, 31)])
        here = (rows_at(x * 8 + z, 16), half) if whole else (x * 8 + z,)
        landed = {kx: arrival() for kx in X_ORDER} if whole else dict.fromkeys(X_ORDER, arrival())
        for kx in (2, 1, 3, 0):
            px = lax.rem(x + kx, 4)
            for kz in far_z + (0,):
                if kx == 0 and kz == 0:
                    continue
                pz = lax.rem(z + kz, 8)
                send(src.at[px * 4 + lax.rem(pz, 4)], recv.at[here], sent, landed[kx], dev(px, y, pz))
        recv[here] = src[x * 4 + zl]
        return landed

    row = iota((256, 256), 0)
    col = iota((256, 256), 1)
    perm[0] = ((row // 2 % 8) * 32 + (row // 16) * 2 + row % 2 == col).astype(BF16)
    perm[1] = ((col // 2 % 8) * 32 + (col // 16) * 2 + col % 2 == row).astype(BF16)

    load_rows.wait()
    for xh in range(4):
        for k in range(4):
            at = rows_at(xh * 8 + lax.rem(z + 7 + k, 8), 16)
            sp_n[pl.ds((xh * 4 + k) * 16, 16), :] = rows_in[at, :].astype(BF16)
    sp_s[0] = dot(perm[1], sp_n[...]).astype(BF16).reshape(8, 32, 128)
    pl.semaphore_wait(barrier, len(peers))

    rows_y = along_y(sp_s.at[0], sp_yr)
    for peer in x_peers:
        pl.semaphore_signal(line_sem, inc=1, device_id=peer, device_id_type=MESH)
    load_acc.wait()
    for xh in range(4):
        for k in range(4):
            at = rows_at(xh * 8 + lax.rem(z + 7 + k, 8), 16)
            ac_n[pl.ds((xh * 4 + k) * 16, 16), :] = acc_in[at, :].astype(BF16)
    ac_s[0] = dot(perm[1], ac_n[...]).astype(BF16).reshape(8, 32, 128)
    accs_y = along_y(ac_s.at[0], ac_yr)

    wide = iota((256, 512), 1)
    tall = iota((256, 512), 0)
    xz = tall // 2 % 16
    from_row = (wide // 128 == xz // 4) & (wide // 16 % 4 == xz % 4) & (wide % 16 == (tall // 32) * 2 + tall % 2)
    perm_sum[...] = from_row.astype(BF16)

    load_move.wait()
    chain = (natural(iota((128, 256), 1) // 2) == iota((128, 256), 0)).astype(BF16)
    for t in range(STRATA):
        move = move_ref[pl.ds(t, 1), :]
        to = (move == natural(iota((256, 128), 0) // 2)).astype(BF16)
        stands = jnp.where(row % 2 == col % 2, dot(to, chain), 0.0)
        onehot[t] = stands.astype(BF16)
        if t + 1 < STRATA:
            onehot_t[t] = jnp.transpose(stands).astype(BF16)
            chain = dot((move == iota((128, 128), 0)).astype(BF16), chain).astype(BF16)

    def sort_words(t):
        load_bits[t].wait()
        cat[:, 0:128] = words[t].reshape(512, 128).astype(F32).astype(BF16)
        spread = (iota((32, 512), 1) // 16 == iota((32, 512), 0)).astype(BF16)
        slots = jnp.broadcast_to(list_ref[t, 0].astype(F32).astype(BF16), (8, 32))
        slot_of = dot(slots, spread)[0:1, :].astype(jnp.int32)
        lane = iota((1, 512), 1)
        slot_of = jnp.where(lane // 16 < count_ref[0, t], slot_of * 16 + lane % 16, -1)
        for a in range(4):
            pick = (slot_of == iota((128, 512), 0) + a * 128).astype(BF16)
            got = dot(pick, cat[...])
            wsort[pl.ds(a * 128, 128), :] = got[:, 0:128].astype(jnp.int32)
            usort[pl.ds(a * 128, 128), :] = got[:, 128:256]

    def fill_mask():
        shift = iota((8, 128), 0)

        def one_slot(slot, carry):
            base = slot * 16
            at_row = pl.multiple_of(lax.rem(slot, 4) * 128, 128)
            at_col = pl.multiple_of((slot // 4) * 128, 128)
            on = jnp.broadcast_to(usort[pl.ds(base, 1), :], (8, 128))
            for w in range(0, 16, 2):
                both = []
                for v in (w, w + 1):
                    line = jnp.broadcast_to(wsort[pl.ds(base + v, 1), :], (8, 128))
                    bit = jnp.bitwise_and(jnp.right_shift(line, shift), 1).astype(F32)
                    both.append(on + 2.0 * bit)
                mask[pl.ds(at_row + w * 8, 16), pl.ds(at_col, 128)] = jnp.concatenate(both, axis=0).astype(BF16)
            return carry

        lax.fori_loop(0, 32, one_slot, 0)

    rows_y()
    pl.semaphore_wait(line_sem, len(x_peers))
    sp_s[1] = dot(perm[0], sp_yr[...].reshape(256, 128)).astype(BF16).reshape(8, 32, 128)
    rows_z = to_homes(sp_s.at[1].reshape(16, 16, 128), sp_zr)
    accs_y()
    ac_s[1] = dot(perm[0], ac_yr[...].reshape(256, 128)).astype(BF16).reshape(8, 32, 128)
    accs_z = to_homes(ac_s.at[1].reshape(16, 16, 128), ac_zr)

    cat[:, 128:256] = jnp.ones((512, 128), BF16)
    load_list.wait()
    sort_words(0)
    load_user.wait()
    xl[...] = xs[...].astype(BF16)
    load_uacc.wait()
    eye = iota((128, 128), 0) == iota((128, 128), 1)
    for a in range(8):
        line = jnp.broadcast_to(uacc_ref[pl.ds(a, 1), :], (128, 128))
        ucol[pl.ds(a * 128, 128), :] = jnp.sum(jnp.where(eye, line, 0.0), axis=1, keepdims=True)

    rows_z()
    yh[...] = dot(perm[1], sp_zr[...].reshape(256, 128))

    for t in range(STRATA):
        last = t == STRATA - 1
        rate = RATE_START * RATE_DECAY**t
        ou_s[t, 0] = dot(onehot[t], yh[...].astype(BF16)).astype(BF16).reshape(8, 32, 128)
        out_y = along_y(ou_s.at[t, 0], ou_yr.at[t])
        if last:
            fa_s[0] = dot(onehot[t], ah[...].astype(BF16)).astype(BF16).reshape(8, 32, 128)
            fa_y = along_y(fa_s.at[0], fa_yr)
        if t == 0:
            fill_mask()
        out_y()
        ou_s[t, 1] = dot(perm[0], ou_yr[t].reshape(256, 128)).astype(BF16).reshape(8, 32, 128)
        landed = to_positions(ou_s.at[t, 1].reshape(16, 16, 128), yl.at[t], True)
        if t == 0:
            accs_z()
            ah[...] = dot(perm[1], ac_zr[...].reshape(256, 128))
        if last:
            fa_y()
            fa_s[1] = dot(perm[0], fa_yr[...].reshape(256, 128)).astype(BF16).reshape(8, 32, 128)
            fa_z = to_positions(fa_s.at[1].reshape(16, 16, 128), fa_zr, False)

        chunk = {kx: rows_at(lax.rem(x + 4 - kx, 4), 128) for kx in X_ORDER}
        over_sent, over = take(yl.at[t, :, 0:128]), {kx: arrival() for kx in X_ORDER}
        swap_sent, swap = take(bk_cr.at[t]), {kx: arrival() for kx in X_ORDER}

        def forward(kx):
            wait(yl.at[t, pl.ds(0, 128 if kx else 112), pl.ds(0, 128)], landed[kx])
            mine = yl.at[t, chunk[kx], half]
            send(mine, mine, over_sent, over[kx], other_core)

        def compute(kx):
            at = chunk[kx]
            wait(yl.at[t, pl.ds(0, 128), pl.ds(0, 128)], over[kx])
            scores = lax.dot_general(yl[t, at, :], xl[...], NT, preferred_element_type=F32)
            weight = mask[at, :].astype(F32)
            e = (weight * (scores - jnp.where(weight > 2.0, 1.0, 0.0))).astype(BF16)
            err[at, :] = e
            part[t, at, :] = dot(e, xl[...])
            send(part.at[t, at, other_half], bk_cr.at[t, at], swap_sent, swap[kx], other_core)

        if not last:
            back_sent, back_landed = take(bk_zr.at[t, pl.ds(0, 31)]), arrival()
        else:
            cross_sent, cross = take(fin_r), {kx: arrival() for kx in X_ORDER}

        def go_back(kx):
            at = chunk[kx]
            wait(bk_cr.at[t, pl.ds(0, 128)], swap[kx])
            total = (part[t, at, half] + bk_cr[t, at]).astype(BF16)
            if last:
                fin_s[at, :] = total
                send(fin_s.at[at], fin_r.at[at], cross_sent, cross[kx], other_zh)
                return
            hx = lax.rem(x + 4 - kx, 4)
            bk_z[t, pl.ds(hx * 8, 8)] = total.reshape(8, 16, 128)
            for kz in far_z + (0,):
                pz = lax.rem(z + kz, 8)
                if kx == 0 and kz == 0:
                    bk_zr[t, x * 8 + z] = bk_z[t, x * 8 + z]
                else:
                    send(bk_z.at[t, hx * 8 + pz], bk_zr.at[t, x * 8 + z], back_sent, back_landed, dev(hx, y, pz))

        forward(0)
        forward(1)
        compute(0)
        forward(3)
        compute(1)
        go_back(0)
        forward(2)
        compute(3)
        go_back(1)
        compute(2)
        go_back(3)
        go_back(2)

        def users():
            for u in range(4):
                at = pl.ds(u * 256, 256)
                old = xs[at, :]
                grad = lax.dot_general(err[:, u * 256 : u * 256 + 256], yl[t], TN, preferred_element_type=F32)
                grad = grad + SHRINKAGE * old
                acc = ucol[at, :] + jnp.sum(grad * grad, axis=1, keepdims=True) * (1.0 / 256.0)
                ucol[at, :] = acc
                new = old - grad * (rate / jnp.sqrt(acc))
                xs[at, :] = new
                if not last:
                    xl[at, :] = new.astype(BF16)

        users()
        if not last:
            wait(bk_zr.at[t, pl.ds(0, 31)], back_landed)
            bk_s[t] = dot(perm_sum[...], bk_zr[t].reshape(512, 128)).astype(BF16).reshape(8, 32, 128)
            back_y = along_y(bk_s.at[t], bk_yr.at[t])
            sort_words(t + 1)
            fill_mask()
            back_y()
            grad = dot(onehot_t[t], bk_yr[t].reshape(256, 128)) + SHRINKAGE * yh[...]
            acc = ah[...] + grad * grad
            ah[...] = acc
            yh[...] = yh[...] - rate * grad / jnp.sqrt(acc)
        else:
            store = pltpu.make_async_copy(xs, user_out, local_sem.at[len(loads)])
            store.start()
            wait(fa_zr.at[pl.ds(0, 31)], fa_z[0])
            new_sent, new_landed = take(items_new.at[:, 0:128]), arrival()
            for kx in X_ORDER:
                at = chunk[kx]
                wait(fin_r.at[pl.ds(0, 128)], cross[kx])
                old = yl[t, at, half].astype(F32)
                grad = fin_s[at, :].astype(F32) + fin_r[at, :].astype(F32) + SHRINKAGE * old
                before = fa_zr[pl.ds(lax.rem(x + 4 - kx, 4) * 8, 8)].reshape(128, 128).astype(F32)
                items_new[at, half] = old - rate * grad / jnp.sqrt(before + grad * grad)
                mine = items_new.at[at, half]
                send(mine, mine, new_sent, new_landed, other_core)
            wait(items_new.at[:, 0:128], new_landed)
            done = pltpu.make_async_copy(items_new, item_out, local_sem.at[len(loads) + 1])
            done.start()
            for k, ref in enumerate(sends):
                wait(ref, send_sem.at[k])
            store.wait()
            done.wait()


def on_device(
    user_rows, user_accum, item_rows, item_accum, move_lists, tile_lists, tile_counts, rating_bits
):
    smem, anywhere = pl.BlockSpec(memory_space=pltpu.SMEM), pl.BlockSpec(memory_space=pl.ANY)
    v = pltpu.VMEM
    by_y, by_xz = (8, 32, 128), (16, 16, 128)
    new_users, new_items = pl.pallas_call(
        kernel,
        out_shape=(
            jax.ShapeDtypeStruct((1024, 256), F32),
            jax.ShapeDtypeStruct((512, 256), F32),
        ),
        in_specs=[anywhere, anywhere, anywhere, anywhere, anywhere, anywhere, smem, anywhere],
        out_specs=(anywhere, anywhere),
        scratch_shapes=[
            v((1024, 256), F32), v((1024, 256), BF16), v((8, 128), F32), v((1024, 1), F32),
            v((STRATA, 128), jnp.int32), v((STRATA, 1, 1, 32), jnp.int32),
            v((STRATA, 32, 16, 128), jnp.int32), v((512, 256), BF16), v((512, 128), jnp.int32), v((512, 128), F32),
            v((512, 1024), BF16), v((512, 1024), BF16), v((STRATA, 512, 256), BF16), v((STRATA, 512, 256), F32),
            v((256, 128), F32), v((256, 128), F32),
            v((STRATA, 256, 256), BF16), v((2, 256, 256), BF16), v((2, 256, 256), BF16), v((256, 512), BF16),
            v((512, 128), F32), v((512, 128), F32), v((512, 256), F32),
            v((256, 128), BF16), v((2, *by_y), BF16), v(by_y, BF16), v(by_xz, BF16),
            v((256, 128), BF16), v((2, *by_y), BF16), v(by_y, BF16), v(by_xz, BF16),
            v((STRATA, 2, *by_y), BF16), v((STRATA, *by_y), BF16),
            v((2, *by_y), BF16), v(by_y, BF16), v((32, 16, 128), BF16),
            v((STRATA, 512, 128), F32), v((2, 32, 16, 128), BF16), v((2, 32, 16, 128), BF16),
            v((2, *by_y), BF16), v((2, *by_y), BF16),
            v((512, 128), BF16), v((512, 128), BF16),
            pltpu.SemaphoreType.DMA((12,)),
            pltpu.SemaphoreType.DMA((24,)),
            pltpu.SemaphoreType.DMA((64,)),
            pltpu.SemaphoreType.REGULAR,
        ],
        compiler_params=pltpu.CompilerParams(
            collective_id=0, has_side_effects=True, vmem_limit_bytes=60 * 1024 * 1024
        ),
        cost_estimate=pl.CostEstimate(flops=3 * 3 * 2 * 1024 * 512 * 256, bytes_accessed=6 * 1024 * 1024, transcendentals=0),
    )(
        user_rows, user_accum.reshape(8, 128), item_rows, item_accum, move_lists, tile_lists,
        tile_counts.transpose(1, 2, 0).reshape(1, STRATA), rating_bits,
    )
    return new_users, new_items


def solution(mesh):
    in_specs = (
        P(("stratum", "rep"), None),
        P(("stratum", "rep")),
        P("stratum", None),
        P("stratum", None),
        P(),
        P(None, "stratum", "rep", None),
        P(None, "stratum", "rep"),
        P(None, "stratum", "rep", None, None, None),
    )
    out_specs = (P(("stratum", "rep"), None), P("stratum", None))
    return jax.shard_map(
        on_device, mesh=mesh, in_specs=in_specs, out_specs=out_specs, check_vma=False
    )
```
